32 devices in a mesh: groups: 2 (over x), blk: 16 (over z, y, core).
Axes of the slice: x: 2, y: 2, z: 4, core: 2. Of those that a mesh axis runs over, the one named last changes fastest.
Arguments:
- tokens: bfloat16 [8192, 4096], P(('groups', 'blk')), parts along dimension 0, may hold values from -6 to 6
- expert_ids: int32 [8192, 8], P(('groups', 'blk')), parts along dimension 0, may hold values from 0 to 127, all different within a row; in each aligned block of 256 rows (0 to 255, 256 to 511, ...) at most 32 rows name the same one
- route_prob: float32 [8192, 8], P(('groups', 'blk')), parts along dimension 0, may hold values from 0.05 to 0.6
- gate_up: bfloat16 [2, 6144, 4096], P(None, 'blk'), may hold values from -0.09375 to 0.09375
- block_scale: float32 [2, 48, 32], P(None, 'blk'), may hold values from 0.25 to 3
Outputs:
- slot_hidden: bfloat16 [1024, 6144], P(('groups', 'blk')), parts along dimension 0
The draws below stay inside these ranges and needn't reach their ends.
There are 2 independent parts, one for each index of `groups`. The reference program is written for one: setup_inputs(seed, part) draws one part's arguments, and reference() takes and returns one part's arrays. A program takes and returns all parts, laid end to end along the dimension named above; an argument that names none is the same for every part. Nothing has to cross between parts.
Inputs may be any that keep to these rules, and one draw needn't show every extreme that they name: `expert_ids`: each row names 8 different experts. Within the 256 rows of one device no expert is named more than 32 times, a bound that some block reaches.
All inputs are finite; a program needn't handle non-finite values.
Results may differ from the reference program's by a relative error of at most 0.0058.
Values may be sent and summed in bfloat16 or wider, within the bound.
A program may use at most 192 MiB of HBM per device.

```python
import math
import jax
import jax.numpy as jnp
import numpy as np
from jax import lax

D = 4096
EXPERTS = 128
TOP = 8
FF = 1536
QB = 128
TOK_DEV = 256
CAP = 32
EW = 4
TOKENS = 4096
N_BLK = 16


def levels(own_key, dims, split, least, top_value):
    def one(dim, shards_of):
        heights = jax.random.uniform(jax.random.fold_in(jax.random.fold_in(own_key, 6), dim), (shards_of,), jnp.float32, least / len(split), top_value / len(split))
        return jnp.repeat(jnp.exp(heights), dims[dim] // shards_of).reshape((-1,) + (1,) * (len(dims) - dim - 1))

    gain = one(*split[0])
    for cut in split[1:]:
        gain = gain * one(*cut)
    return gain


def assign_block(stream_key, own, number, rows, count, top, limit, slope):
    sequence = jax.random.permutation(stream_key, count)
    packed, common = load_shares(count, rows * top, limit, slope, True), load_shares(count, rows * top, limit, slope, False)
    places = jnp.arange(count)

    def named(sizes, rotation):
        used = int((sizes > 0).sum())
        fixed = max(1, used // 4)
        passed = fixed + (places - fixed + rotation * (used - fixed)) % max(1, count - fixed)
        return jnp.zeros((count,), jnp.int32).at[sequence[jnp.where(places < fixed, places, passed)]].set(jnp.asarray(sizes, jnp.int32))

    sizes = jnp.where(number % 4 == 0, named(packed, number // 4), named(common, number - number // 4 - 1))
    mixed = jax.random.permutation(jax.random.fold_in(own, 3), count)
    source_of, receiver = mixed[0:count // 2 * 2:2], mixed[1:count // 2 * 2:2]
    margin = jnp.minimum(sizes[source_of] - 1, limit - sizes[receiver]) // 2
    margin = jnp.where((source_of == sequence[0]) | (receiver == sequence[0]) | (sizes[receiver] == 0), 0, jnp.maximum(margin, 0))
    passed = jax.random.randint(jax.random.fold_in(own, 4), (count // 2,), 0, 1 << 20) % (margin + 1)
    sizes = sizes.at[source_of].add(-passed).at[receiver].add(passed)
    members = jnp.searchsorted(jnp.cumsum(sizes), jnp.arange(rows * top), side="right").astype(jnp.int32)
    listing = members.reshape(top, rows).T
    listing = listing[jax.random.permutation(jax.random.fold_in(own, 1), rows)]
    rotation = jax.random.randint(jax.random.fold_in(own, 2), (rows, 1), 0, top)
    return jnp.take_along_axis(listing, (jnp.arange(top)[None, :] + rotation) % top, axis=1)


def load_shares(amount, total, limit, skew, full):
    weights = [(1 << 20) // math.isqrt(grade ** skew) + 1 for grade in range(1, amount + 1)]
    largest = limit if full else min(limit, max(-(-total // amount), total * weights[0] // sum(weights)))
    least = 1 if total - largest >= amount - 1 else 0
    counts, rest = [largest] + [least] * (amount - 1), total - largest - least * (amount - 1)
    while rest > 0:
        candidates = [i for i in range(1, amount) if counts[i] < largest] or [i for i in range(1, amount) if counts[i] < limit]
        whole, budget = sum([weights[i] for i in candidates]), rest
        for i in candidates:
            extra = min(limit - counts[i], max(1, budget * weights[i] // whole), rest)
            counts[i] = counts[i] + extra
            rest = rest - extra
    return np.array(counts)


def scatter_about(own_key, dims, deviation, limit, cuts=(), kind=jnp.bfloat16):
    factor_of = levels(own_key, dims, cuts, -0.22, 0.18) if cuts else 1.0
    result = jax.random.normal(own_key, dims, jnp.float32) * deviation * factor_of
    return jnp.minimum(jnp.maximum(result, -limit), limit).astype(kind)


def setup_inputs(seed: int = 0, part: int = 0) -> dict:
    keys = jax.random.split(jax.random.key(seed), 6)
    part_keys = jax.random.split(jax.random.fold_in(keys[5], part), 6)
    tokens = scatter_about(part_keys[0], (TOKENS, D), 1.0, 6.0, ((0, 16),))
    expert_ids_keys = jax.random.split(jax.random.fold_in(part_keys[1], 1), TOKENS // TOK_DEV)
    expert_ids_turns = jax.random.permutation(jax.random.fold_in(part_keys[1], 3), TOKENS // TOK_DEV)
    expert_ids = jax.vmap(lambda own, number: assign_block(jax.random.fold_in(part_keys[1], 2), own, number, TOK_DEV, EXPERTS, TOP, CAP, 1))(expert_ids_keys, expert_ids_turns).reshape((TOKENS, TOP))
    route_prob = jnp.clip(0.05 + 0.55 * jax.random.uniform(part_keys[2], (TOKENS, TOP), jnp.float32) ** levels(part_keys[2], (TOKENS, TOP), ((0, 16),), -0.2, 0.2), 0.05, 0.6)
    gate_up = scatter_about(keys[3], (2, EW * FF, D), D ** -0.5, 0.09375, ((1, 16),))
    block_scale = jnp.clip(jnp.exp(math.log(3.0) - 2.4849066 * jax.random.uniform(keys[4], (2, EW * FF // QB, D // QB), jnp.float32) ** levels(keys[4], (2, EW * FF // QB, D // QB), ((1, 16),), -0.2, 0.2)), 0.25, 3.0)
    return {"tokens": tokens, "expert_ids": expert_ids, "route_prob": route_prob, "gate_up": gate_up, "block_scale": block_scale}


def dequantize(gate_up, block_scale):
    expanded = jnp.repeat(jnp.repeat(block_scale, QB, axis=1), QB, axis=2)
    return (gate_up.astype(jnp.float32) * expanded).astype(jnp.bfloat16)


def slot_table(expert_ids, route_prob, count):
    window = jnp.arange(count, dtype=jnp.int32)
    match = expert_ids[:, :, None] == window[None, None, :]
    routed = jnp.any(match, axis=1)
    share = jnp.sum(jnp.where(match, route_prob[:, :, None], jnp.float32(0.0)), axis=1).astype(jnp.float32)
    rank = (jnp.cumsum(routed.astype(jnp.int32), axis=0) - 1).astype(jnp.int32)
    positions = jnp.arange(CAP, dtype=jnp.int32)
    chosen = routed[None] & (rank[None] == positions[:, None, None])
    token_iota = jnp.arange(expert_ids.shape[0], dtype=jnp.int32)
    slot_token = jnp.sum(jnp.where(chosen, token_iota[None, :, None], 0), axis=1).astype(jnp.int32).T
    slot_share = jnp.sum(jnp.where(chosen, share[None], jnp.float32(0.0)), axis=1).astype(jnp.float32).T
    return slot_token, slot_share


def reference(tokens, expert_ids, route_prob, gate_up, block_scale):
    weights = dequantize(gate_up, block_scale).astype(jnp.float32).reshape(2, EW, FF, D)

    def one_block(inputs):
        local_tokens, local_ids, local_prob = inputs
        slot_token, slot_share = slot_table(local_ids, local_prob, EW)
        slot_rows = local_tokens[slot_token].astype(jnp.float32)
        proj = jnp.einsum("ecd,pefd->pecf", slot_rows, weights)
        act = jax.nn.silu(proj[0]) * proj[1]
        value = slot_share[:, :, None] * act
        return jnp.transpose(value, (1, 0, 2)).reshape(CAP, EW * FF).astype(jnp.bfloat16)

    blocks = lax.map(one_block, (tokens.reshape(N_BLK, TOK_DEV, D), expert_ids.reshape(N_BLK, TOK_DEV, TOP), route_prob.reshape(N_BLK, TOK_DEV, TOP)))
    return blocks.reshape(N_BLK * CAP, EW * FF)
```

```python
import functools

import jax
import jax.numpy as jnp
from jax import lax
from jax.experimental import pallas as pl
from jax.experimental.pallas import tpu as pltpu
from jax.sharding import PartitionSpec as P

SPLIT = 4
QB = 128
CAP = 32
F32 = jnp.float32
BF16 = jnp.bfloat16


def xor(v, s):
    out, bit = v, 1
    while bit <= s:
        if s & bit:
            out = out + bit - 2 * bit * lax.rem(lax.div(v, bit), 2)
        bit *= 2
    return out


def kernel(n, parts, ids_ref, prob_ref, scale_ref, tok_hbm, w_hbm, out_ref,
           tok, w, tx, rx, hid, ret, share,
           load_sem, z_send, z_recv, y_send, y_recv, a_send, a_recv, b_send, b_recv, r_send, r_recv):
    quads = n // SPLIT
    tokens, depth = tok.shape
    width = depth // parts
    tiles = w.shape[0]
    me = lax.axis_index("blk")
    quad, member = lax.div(me, SPLIT), lax.rem(me, SPLIT)

    def remote(src, dst, send, recv, target):
        copy = pltpu.make_async_remote_copy(
            src_ref=src, dst_ref=dst, send_sem=send, recv_sem=recv,
            device_id={"blk": target}, device_id_type=pl.DeviceIdType.MESH)
        copy.start()
        started.append(copy)
        return copy

    started = []
    load_tokens = pltpu.make_async_copy(tok_hbm, tok, load_sem.at[0])
    load_tokens.start()
    barrier = pltpu.get_barrier_semaphore()
    for step in range(1, n):
        pl.semaphore_signal(barrier, inc=1, device_id={"blk": lax.rem(me + step, n)},
                            device_id_type=pl.DeviceIdType.MESH)
    loads = []
    for t in range(tiles):
        for proj in range(2):
            load = pltpu.make_async_copy(
                w_hbm.at[proj, pl.ds(t * QB, QB)], w.at[t, pl.ds(proj * QB, QB)],
                load_sem.at[1 + 2 * t + proj])
            load.start()
            loads.append(load)

    slots = quads * CAP
    lane = lax.broadcasted_iota(jnp.int32, (tokens, slots), 1)
    expert, place = lane // CAP, lane % CAP
    routed = jnp.zeros((tokens, slots), F32)
    portion = jnp.zeros((tokens, slots), F32)
    for j in range(ids_ref.shape[1]):
        hit = ids_ref[:, j:j + 1] == expert
        routed = jnp.where(hit, F32(1), routed)
        portion = jnp.where(hit, prob_ref[:, j:j + 1], portion)
    earlier = lax.broadcasted_iota(jnp.int32, (tokens, tokens), 1) <= lax.broadcasted_iota(
        jnp.int32, (tokens, tokens), 0)
    count = jnp.dot(jnp.where(earlier, F32(1), F32(0)).astype(BF16), routed.astype(BF16),
                    preferred_element_type=F32)
    chosen = jnp.where(count == (place + 1).astype(F32), routed, F32(0))
    pick = chosen.T.astype(BF16)

    load_tokens.wait()

    def gather(k):
        rows = jnp.dot(pick, tok[:, k * width:(k + 1) * width], preferred_element_type=F32).astype(BF16)
        for e in range(quads):
            tx[e, k] = rows[e * CAP:(e + 1) * CAP]

    def send_z(s, k):
        there = xor(quad, s)
        zs[s, k] = remote(tx.at[there, k], rx.at[me, k], z_send.at[s, k], z_recv.at[s, k],
                          there * SPLIT + member)

    def send_quad(s, k, source):
        block = xor(quad, s) * SPLIT + member
        base = quad * SPLIT
        ys[s, k] = remote(source, rx.at[block, k], y_send.at[s, k], y_recv.at[s, k],
                          base + xor(member, 2))
        near[s, k] = remote(source, rx.at[block, k], a_send.at[s, k], a_recv.at[s, k],
                            base + xor(member, 1))

    def arrived_z(s, k):
        zs[s, k].wait_recv()
        send_quad(s, k, rx.at[xor(quad, s) * SPLIT + member, k])

    def arrived_y(s, k):
        ys[s, k].wait_recv()
        block = xor(quad, s) * SPLIT + xor(member, 2)
        far[s, k] = remote(rx.at[block, k], rx.at[block, k], b_send.at[s, k], b_recv.at[s, k],
                           quad * SPLIT + xor(member, 1))

    def scale_weights(index):
        t, proj = index // 2, index % 2
        loads[index].wait()

        def body(kb, carry):
            where = (t, pl.ds(proj * QB, QB), pl.ds(pl.multiple_of(kb * QB, QB), QB))
            w[where] = (w[where].astype(F32) * scale_ref[proj, t, kb]).astype(BF16)
            return carry

        lax.fori_loop(0, depth // QB, body, 0, unroll=4)

    def compute(s):
        there = xor(quad, s)
        for k in range(parts):
            near[s, k].wait_recv()
            far[s, k].wait_recv()
        first = there * SPLIT

        def body(t, carry):
            x = jnp.concatenate(
                [rx[pl.ds(first, SPLIT), k].reshape(SPLIT * CAP, width) for k in range(parts)], axis=1)
            both = lax.dot_general(x, w[t], (((1,), (1,)), ((), ())), preferred_element_type=F32)
            gate, up = both[:, :QB], both[:, QB:]
            act = (gate / (F32(1) + jnp.exp(-gate)) * up).astype(BF16)
            hid[pl.ds(first, SPLIT), t] = act.reshape(SPLIT, CAP, QB)
            return carry

        lax.fori_loop(0, tiles, body, 0)
        for r in range(SPLIT):
            if s or r:
                target = first + xor(member, r)
                back[s, r] = remote(hid.at[target], ret.at[me], r_send.at[s, r], r_recv.at[s, r], target)

    def finish(s):
        there = xor(quad, s)
        scale = share[pl.ds(pl.multiple_of(there * CAP, CAP), CAP), :]
        for r in range(SPLIT):
            source = there * SPLIT + xor(member, r)
            if s or r:
                back[s, r].wait_recv()
            for t in range(tiles):
                act = ret[source, t] if s or r else hid[source, t]
                at = pl.multiple_of((source * tiles + t) * QB, QB)
                out_ref[:, pl.ds(at, QB)] = (scale * act.astype(F32)).astype(BF16)

    zs, ys, near, far, back = {}, {}, {}, {}, {}
    lead = [quads // 2, 1]
    order = [(s, k) for k in range(parts) for s in lead]
    order += [(s, k) for s in range(1, quads) if s not in lead for k in range(parts)]
    window = 2 * parts

    pl.semaphore_wait(barrier, n - 1)
    for k in range(parts):
        gather(k)
        for s, piece in order[:window]:
            if piece == k:
                send_z(s, k)
        send_quad(0, k, tx.at[quad, k])
    own = pltpu.make_async_copy(tx.at[quad], rx.at[me], load_sem.at[0])
    own.start()
    part_share = jnp.sum((chosen * portion).T, axis=1, keepdims=True)
    share[...] = jnp.broadcast_to(part_share, share.shape)

    todo = [functools.partial(scale_weights, i) for i in range(2 * tiles)]
    for k in range(parts):
        todo.pop(0)()
        arrived_y(0, k)
    own.wait()

    left = {s: parts for s in range(1, quads)}
    ready, done = [0], []
    lag = 2
    behind = []
    for i, (s, k) in enumerate(order):
        arrived_z(s, k)
        if i + window < len(order):
            send_z(*order[i + window])
        behind.append((s, k))
        while todo and i % 2 == 1:
            todo.pop(0)()
            break
        if len(behind) > lag or i == len(order) - 1:
            while len(behind) > (lag if i < len(order) - 1 else 0):
                late = behind.pop(0)
                arrived_y(*late)
                left[late[0]] -= 1
                if left[late[0]] == 0:
                    ready.append(late[0])
        if i == len(order) - 1:
            while todo:
                todo.pop(0)()
        if not todo:
            while ready:
                s_now = ready.pop(0)
                compute(s_now)
                done.append(s_now)
    for s in done:
        finish(s)
    for copy in started:
        copy.wait_send()


def local(n, ids, prob, scale, tokens, gate_up):
    quads = n // SPLIT
    parts = max(2, 16 // quads)
    count, depth = tokens.shape
    tiles = gate_up.shape[1] // QB
    dma = pltpu.SemaphoreType.DMA
    vmem = pl.BlockSpec(memory_space=pltpu.VMEM)
    hbm = pl.BlockSpec(memory_space=pl.ANY)
    return pl.pallas_call(
        functools.partial(kernel, n, parts),
        out_shape=jax.ShapeDtypeStruct((CAP, n * tiles * QB), BF16),
        in_specs=[vmem, vmem, pl.BlockSpec(memory_space=pltpu.SMEM), hbm, hbm],
        out_specs=vmem,
        scratch_shapes=[
            pltpu.VMEM((count, depth), BF16),
            pltpu.VMEM((tiles, 2 * QB, depth), BF16),
            pltpu.VMEM((quads, parts, CAP, depth // parts), BF16),
            pltpu.VMEM((n, parts, CAP, depth // parts), BF16),
            pltpu.VMEM((n, tiles, CAP, QB), BF16),
            pltpu.VMEM((n, tiles, CAP, QB), BF16),
            pltpu.VMEM((quads * CAP, QB), F32),
            dma((1 + 2 * tiles,)),
        ] + [dma((quads, parts))] * 8 + [dma((quads, SPLIT))] * 2,
        compiler_params=pltpu.CompilerParams(
            collective_id=0, has_side_effects=True, vmem_limit_bytes=56 * 1024 * 1024),
        cost_estimate=pl.CostEstimate(
            flops=2 * n * CAP * 2 * tiles * QB * depth, bytes_accessed=10 ** 7, transcendentals=0),
    )(ids, prob, scale, tokens, gate_up)


def solution(mesh):
    n = mesh.shape["blk"]
    placed = (
        P(("groups", "blk"), None),
        P(("groups", "blk"), None),
        P(("groups", "blk"), None),
        P(None, "blk", None),
        P(None, "blk", None),
    )

    def body(tokens, expert_ids, route_prob, gate_up, block_scale):
        return local(n, expert_ids, route_prob, block_scale, tokens, gate_up)

    return jax.shard_map(
        body, mesh=mesh, in_specs=placed, out_specs=P(("groups", "blk"), None), check_vma=False
    )
```

```python
import functools

import jax
import jax.numpy as jnp
from jax import lax
from jax.experimental import pallas as pl
from jax.experimental.pallas import tpu as pltpu
from jax.sharding import PartitionSpec as P

SPLIT = 4
QB = 128
CAP = 32
HALF = CAP // 2
WINDOW = 4
LAG = 4
BEFORE = 4
F32 = jnp.float32
BF16 = jnp.bfloat16


def xor(v, s):
    out, bit = v, 1
    while bit <= s:
        if s & bit:
            out = out + bit - 2 * bit * lax.rem(lax.div(v, bit), 2)
        bit *= 2
    return out


def kernel(n, parts, ids_ref, prob_ref, scale_ref, tok_hbm, w_hbm, out_ref,
           tok, w, tx, rx, hid, ret, share, load_sem, sent, z_recv, y_recv, near_recv, far_recv, r_recv):
    quads = n // SPLIT
    tokens, depth = tok.shape
    width = depth // parts
    tiles = w.shape[0]
    me = lax.axis_index("blk")
    quad, member = lax.div(me, SPLIT), lax.rem(me, SPLIT)
    chunks = [(h, c) for h in range(2) for c in range(parts)]

    barrier = pltpu.get_barrier_semaphore()
    for step in range(1, n):
        pl.semaphore_signal(barrier, inc=1, device_id={"blk": lax.rem(me + step, n)},
                            device_id_type=pl.DeviceIdType.MESH)
    load_tokens = pltpu.make_async_copy(tok_hbm, tok, load_sem.at[0])
    load_tokens.start()
    loads = []
    for t in range(tiles):
        for proj in range(2):
            load = pltpu.make_async_copy(
                w_hbm.at[proj, pl.ds(t * QB, QB)], w.at[t, pl.ds(proj * QB, QB)],
                load_sem.at[1 + 2 * t + proj])
            load.start()
            loads.append(load)

    def remote(src, dst, send, recv, target):
        copy = pltpu.make_async_remote_copy(
            src_ref=src, dst_ref=dst, send_sem=send, recv_sem=recv,
            device_id={"blk": target}, device_id_type=pl.DeviceIdType.MESH)
        copy.start()
        return copy

    def wait_for(ref, sem):
        pltpu.make_async_copy(ref, ref, sem).wait()

    slots = quads * CAP
    row = lax.broadcasted_iota(jnp.int32, (slots, tokens), 0)
    expert, place = row // CAP, row % CAP
    routed = jnp.zeros((slots, tokens), F32)
    portion = jnp.zeros((slots, tokens), F32)
    for j in range(ids_ref.shape[0]):
        hit = ids_ref[j:j + 1, :] == expert
        routed = jnp.where(hit, F32(1), routed)
        portion = jnp.where(hit, prob_ref[j:j + 1, :], portion)
    earlier = lax.broadcasted_iota(jnp.int32, (tokens, tokens), 0) <= lax.broadcasted_iota(
        jnp.int32, (tokens, tokens), 1)
    count = jnp.dot(routed.astype(BF16), jnp.where(earlier, F32(1), F32(0)).astype(BF16),
                    preferred_element_type=F32)
    chosen = jnp.where(count == (place + 1).astype(F32), routed, F32(0))
    pick = chosen.astype(BF16)
    total = jnp.sum(chosen * portion, axis=1, keepdims=True)
    share[...] = jnp.broadcast_to(total, share.shape)

    load_tokens.wait()
    for c in range(parts):
        rows = jnp.dot(pick, tok[:, c * width:(c + 1) * width], preferred_element_type=F32).astype(BF16)
        for e in range(quads):
            for h in range(2):
                tx[e, h, c] = rows[e * CAP + h * HALF:e * CAP + (h + 1) * HALF]

    def scale_weights(index):
        t, proj = index // 2, index % 2
        loads[index].wait()

        def body(kb, carry):
            where = (t, pl.ds(proj * QB, QB), pl.ds(pl.multiple_of(kb * QB, QB), QB))
            w[where] = (w[where].astype(F32) * scale_ref[t, proj, kb]).astype(BF16)
            return carry

        lax.fori_loop(0, depth // QB, body, 0, unroll=4)

    zs, ys = {}, {}

    def send_z(s, h, c):
        there = xor(quad, s)
        zs[s, h, c] = remote(tx.at[there, h, c], rx.at[me, h, c], sent.at[0], z_recv.at[s, h, c],
                             there * SPLIT + member)

    def send_quad(s, h, c, source):
        block = xor(quad, s) * SPLIT + member
        base = quad * SPLIT
        ys[s, h, c] = remote(source, rx.at[block, h, c], sent.at[1], y_recv.at[s, h, c],
                             base + xor(member, 2))
        remote(source, rx.at[block, h, c], sent.at[2], near_recv.at[s, h], base + xor(member, 1))

    def arrived_z(s, h, c):
        zs[s, h, c].wait_recv()
        send_quad(s, h, c, rx.at[xor(quad, s) * SPLIT + member, h, c])

    def arrived_y(s, h, c):
        ys[s, h, c].wait_recv()
        block = xor(quad, s) * SPLIT + xor(member, 2)
        remote(rx.at[block, h, c], rx.at[block, h, c], sent.at[3], far_recv.at[s, h],
               quad * SPLIT + xor(member, 1))

    def arrived_all(s, halves):
        for h in halves:
            wait_for(rx.at[0, 0], near_recv.at[s, h])
            wait_for(rx.at[0, 0], far_recv.at[s, h])

    def compute(s, halves, t):
        first = pl.ds(xor(quad, s) * SPLIT, SPLIT)
        which = slice(None) if len(halves) == 2 else halves[0]
        count = SPLIT * HALF * len(halves)
        x = jnp.concatenate([rx[first, which, c].reshape(count, width) for c in range(parts)], axis=1)
        both = lax.dot_general(x, w[t], (((1,), (1,)), ((), ())), preferred_element_type=F32)
        gate, up = both[:, :QB], both[:, QB:]
        act = (gate / (F32(1) + jnp.exp(-gate)) * up).astype(BF16)
        if len(halves) == 2:
            hid[first, :, t] = act.reshape(SPLIT, 2, HALF, QB)
        else:
            hid[first, which, t] = act.reshape(SPLIT, HALF, QB)

    def send_back(s, halves):
        for r in range(SPLIT):
            target = xor(quad, s) * SPLIT + xor(member, r)
            if s == 0 and r == 0:
                continue
            elif len(halves) == 2:
                remote(hid.at[target], ret.at[me], sent.at[4], r_recv.at[s], target)
            else:
                h = halves[0]
                remote(hid.at[target, h], ret.at[me, h], sent.at[4], r_recv.at[s], target)

    def finish(s):
        wait_for(ret.at[pl.ds(0, SPLIT if s else SPLIT - 1)], r_recv.at[s])
        there = xor(quad, s)
        for r in range(SPLIT):
            source = there * SPLIT + xor(member, r)
            back = ret if s or r else hid
            for h in range(2):
                scale = share[pl.ds(pl.multiple_of(there * CAP + h * HALF, HALF), HALF), :]
                for t in range(tiles):
                    at = pl.multiple_of((source * tiles + t) * QB, QB)
                    out_ref[h * HALF:(h + 1) * HALF, pl.ds(at, QB)] = (
                        scale * back[source, h, t].astype(F32)).astype(BF16)

    lead = quads // 2
    last = quads - 1
    rest = [s for s in range(1, last) if s != lead]
    order = []
    for h, c in chunks:
        order += [(lead, h, c), (rest[0], h, c)]
    for s in rest[1:] + [last]:
        order += [(s, h, c) for h, c in chunks]

    todo = [functools.partial(scale_weights, i) for i in range(2 * tiles)]
    for _ in range(BEFORE):
        todo.pop(0)()
    own = pltpu.make_async_copy(tx.at[quad], rx.at[me], load_sem.at[0])
    own.start()

    pl.semaphore_wait(barrier, n - 1)
    local_chunks = list(chunks)
    behind = []

    def local_chunk():
        h, c = local_chunks.pop(0)
        send_quad(0, h, c, tx.at[quad, h, c])
        behind.append((0, h, c))

    for i in range(WINDOW):
        send_z(*order[i])
        if i < 2:
            local_chunk()
    while todo:
        todo.pop(0)()
    own.wait()

    left = {}
    for s in range(quads):
        for h in range(2):
            left[s, h] = parts
    issued = [WINDOW]

    def queue(s, halves):
        todo.append(functools.partial(arrived_all, s, halves))
        if quads <= 4:
            todo.extend(functools.partial(compute, s, halves, t) for t in range(tiles))
        else:
            todo.append(lambda: pl.loop(0, tiles)(functools.partial(compute, s, halves)))
        todo.append(functools.partial(send_back, s, halves))

    def take_y():
        s, h, c = behind.pop(0)
        arrived_y(s, h, c)
        left[s, h] -= 1
        if left[s, h] == 0:
            if s == last:
                queue(s, (h,))
            elif left[s, 1 - h] == 0:
                queue(s, (0, 1))

    for i, event in enumerate(order):
        work = len(todo)
        arrived_z(*event)
        behind.append(event)
        while issued[0] < len(order) and issued[0] <= i + WINDOW:
            send_z(*order[issued[0]])
            issued[0] += 1
        if local_chunks:
            local_chunk()
        while len(behind) > LAG:
            take_y()
        for _ in range(min(work, 3)):
            todo.pop(0)()
    while behind:
        take_y()
        if todo:
            todo.pop(0)()
    while todo:
        todo.pop(0)()
    for s in range(quads):
        finish(s)
    wait_for(tx.at[pl.ds(0, quads - 1)], sent.at[0])
    for kind in (1, 2, 3):
        wait_for(tx, sent.at[kind])
    wait_for(hid.at[pl.ds(0, n - 1)], sent.at[4])


def local(n, ids, prob, scale, tokens, gate_up):
    quads = n // SPLIT
    parts = max(1, 8 // quads)
    count, depth = tokens.shape
    tiles = gate_up.shape[1] // QB
    dma = pltpu.SemaphoreType.DMA
    vmem = pl.BlockSpec(memory_space=pltpu.VMEM)
    hbm = pl.BlockSpec(memory_space=pl.ANY)
    chunk = (2, parts, HALF, depth // parts)
    params = dict(vmem_limit_bytes=56 * 1024 * 1024)
    return pl.pallas_call(
        functools.partial(kernel, n, parts),
        out_shape=jax.ShapeDtypeStruct((CAP, n * tiles * QB), BF16),
        in_specs=[vmem, vmem, pl.BlockSpec(memory_space=pltpu.SMEM), hbm, hbm],
        out_specs=vmem,
        scratch_shapes=[
            pltpu.VMEM((count, depth), BF16),
            pltpu.VMEM((tiles, 2 * QB, depth), BF16),
            pltpu.VMEM((quads,) + chunk, BF16),
            pltpu.VMEM((n,) + chunk, BF16),
            pltpu.VMEM((n, 2, tiles, HALF, QB), BF16),
            pltpu.VMEM((n, 2, tiles, HALF, QB), BF16),
            pltpu.VMEM((quads * CAP, QB), F32),
            dma((1 + 2 * tiles,)),
            dma((5,)),
            dma((quads, 2, parts)),
            dma((quads, 2, parts)),
            dma((quads, 2)),
            dma((quads, 2)),
            dma((quads,)),
        ],
        compiler_params=pltpu.CompilerParams(collective_id=0, has_side_effects=True, **params),
        cost_estimate=pl.CostEstimate(
            flops=2 * n * CAP * 2 * tiles * QB * depth, bytes_accessed=10 ** 7, transcendentals=0),
    )(ids.T, prob.T, scale.transpose(1, 0, 2), tokens, gate_up)


def solution(mesh):
    n = mesh.shape["blk"]
    placed = (
        P(("groups", "blk"), None),
        P(("groups", "blk"), None),
        P(("groups", "blk"), None),
        P(None, "blk", None),
        P(None, "blk", None),
    )

    def body(tokens, expert_ids, route_prob, gate_up, block_scale):
        return local(n, expert_ids, route_prob, block_scale, tokens, gate_up)

    return jax.shard_map(
        body, mesh=mesh, in_specs=placed, out_specs=P(("groups", "blk"), None), check_vma=False
    )
```

```python
import functools

import jax
import jax.numpy as jnp
from jax import lax
from jax.experimental import pallas as pl
from jax.experimental.pallas import tpu as pltpu
from jax.sharding import PartitionSpec as P

SPLIT = 4
QB = 128
CAP = 32
HALF = CAP // 2
WINDOW = 4
LAG = 4
BEFORE = 4
F32 = jnp.float32
BF16 = jnp.bfloat16


def xor(v, s):
    out, bit = v, 1
    while bit <= s:
        if s & bit:
            out = out + bit - 2 * bit * lax.rem(lax.div(v, bit), 2)
        bit *= 2
    return out


def kernel(n, parts, ids_ref, prob_ref, scale_ref, tok_hbm, w_hbm, out_ref,
           tok, w, tx, rx, hid, ret, share, load_sem, sent, z_recv, y_recv, near_recv, far_recv, r_recv):
    quads = n // SPLIT
    tokens, depth = tok.shape
    width = depth // parts
    tiles = w.shape[0]
    me = lax.axis_index("blk")
    quad, member = lax.div(me, SPLIT), lax.rem(me, SPLIT)
    chunks = [(h, c) for h in range(2) for c in range(parts)]

    barrier = pltpu.get_barrier_semaphore()
    for step in range(1, n):
        pl.semaphore_signal(barrier, inc=1, device_id={"blk": lax.rem(me + step, n)},
                            device_id_type=pl.DeviceIdType.MESH)
    load_tokens = pltpu.make_async_copy(tok_hbm, tok, load_sem.at[0])
    load_tokens.start()
    loads = []
    for t in range(tiles):
        for proj in range(2):
            load = pltpu.make_async_copy(
                w_hbm.at[proj, pl.ds(t * QB, QB)], w.at[t, pl.ds(proj * QB, QB)],
                load_sem.at[1 + 2 * t + proj])
            load.start()
            loads.append(load)

    def remote(src, dst, send, recv, target):
        copy = pltpu.make_async_remote_copy(
            src_ref=src, dst_ref=dst, send_sem=send, recv_sem=recv,
            device_id={"blk": target}, device_id_type=pl.DeviceIdType.MESH)
        copy.start()
        return copy

    def wait_for(ref, sem):
        pltpu.make_async_copy(ref, ref, sem).wait()

    slots = quads * CAP
    row = lax.broadcasted_iota(jnp.int32, (slots, tokens), 0)
    expert, place = row // CAP, row % CAP
    routed = jnp.zeros((slots, tokens), F32)
    portion = jnp.zeros((slots, tokens), F32)
    for j in range(ids_ref.shape[0]):
        hit = ids_ref[j:j + 1, :] == expert
        routed = jnp.where(hit, F32(1), routed)
        portion = jnp.where(hit, prob_ref[j:j + 1, :], portion)
    earlier = lax.broadcasted_iota(jnp.int32, (tokens, tokens), 0) <= lax.broadcasted_iota(
        jnp.int32, (tokens, tokens), 1)
    count = jnp.dot(routed.astype(BF16), jnp.where(earlier, F32(1), F32(0)).astype(BF16),
                    preferred_element_type=F32)
    chosen = jnp.where(count == (place + 1).astype(F32), routed, F32(0))
    pick = chosen.astype(BF16)
    total = jnp.sum(chosen * portion, axis=1, keepdims=True)
    share[...] = jnp.broadcast_to(total, share.shape)

    load_tokens.wait()
    for c in range(parts):
        rows = jnp.dot(pick, tok[:, c * width:(c + 1) * width], preferred_element_type=F32).astype(BF16)
        for e in range(quads):
            for h in range(2):
                tx[e, h, c] = rows[e * CAP + h * HALF:e * CAP + (h + 1) * HALF]

    def scale_weights(index):
        t, proj = index // 2, index % 2
        loads[index].wait()

        def body(kb, carry):
            where = (t, pl.ds(proj * QB, QB), pl.ds(pl.multiple_of(kb * QB, QB), QB))
            w[where] = (w[where].astype(F32) * scale_ref[t, proj, kb]).astype(BF16)
            return carry

        lax.fori_loop(0, depth // QB, body, 0, unroll=4)

    zs, ys = {}, {}

    def send_z(s, h, c):
        there = xor(quad, s)
        zs[s, h, c] = remote(tx.at[there, h, c], rx.at[me, h, c], sent.at[0], z_recv.at[s, h, c],
                             there * SPLIT + member)

    def send_quad(s, h, c, source):
        block = xor(quad, s) * SPLIT + member
        base = quad * SPLIT
        ys[s, h, c] = remote(source, rx.at[block, h, c], sent.at[1], y_recv.at[s, h, c],
                             base + xor(member, 2))
        remote(source, rx.at[block, h, c], sent.at[2], near_recv.at[s, h], base + xor(member, 1))

    def arrived_z(s, h, c):
        zs[s, h, c].wait_recv()
        send_quad(s, h, c, rx.at[xor(quad, s) * SPLIT + member, h, c])

    def arrived_y(s, h, c):
        ys[s, h, c].wait_recv()
        block = xor(quad, s) * SPLIT + xor(member, 2)
        remote(rx.at[block, h, c], rx.at[block, h, c], sent.at[3], far_recv.at[s, h],
               quad * SPLIT + xor(member, 1))

    def arrived_all(s, halves):
        for h in halves:
            wait_for(rx.at[0, 0], near_recv.at[s, h])
            wait_for(rx.at[0, 0], far_recv.at[s, h])

    def compute(s, halves, t):
        first = pl.ds(xor(quad, s) * SPLIT, SPLIT)
        which = slice(None) if len(halves) == 2 else halves[0]
        count = SPLIT * HALF * len(halves)
        x = jnp.concatenate([rx[first, which, c].reshape(count, width) for c in range(parts)], axis=1)
        both = lax.dot_general(x, w[t], (((1,), (1,)), ((), ())), preferred_element_type=F32)
        gate, up = both[:, :QB], both[:, QB:]
        act = (gate / (F32(1) + jnp.exp(-gate)) * up).astype(BF16)
        if len(halves) == 2:
            hid[first, :, t] = act.reshape(SPLIT, 2, HALF, QB)
        else:
            hid[first, which, t] = act.reshape(SPLIT, HALF, QB)

    def send_back(s, halves):
        for r in range(SPLIT):
            target = xor(quad, s) * SPLIT + xor(member, r)
            if s == 0 and r == 0:
                continue
            elif len(halves) == 2:
                remote(hid.at[target], ret.at[me], sent.at[4], r_recv.at[s], target)
            else:
                h = halves[0]
                remote(hid.at[target, h], ret.at[me, h], sent.at[4], r_recv.at[s], target)

    def finish(s):
        wait_for(ret.at[pl.ds(0, SPLIT if s else SPLIT - 1)], r_recv.at[s])
        there = xor(quad, s)
        for r in range(SPLIT):
            source = there * SPLIT + xor(member, r)
            back = ret if s or r else hid
            for h in range(2):
                scale = share[pl.ds(pl.multiple_of(there * CAP + h * HALF, HALF), HALF), :]
                for t in range(tiles):
                    at = pl.multiple_of((source * tiles + t) * QB, QB)
                    out_ref[h * HALF:(h + 1) * HALF, pl.ds(at, QB)] = (
                        scale * back[source, h, t].astype(F32)).astype(BF16)

    lead = quads // 2
    last = quads - 1
    rest = [s for s in range(1, last) if s != lead]
    order = []
    for h, c in chunks:
        order += [(lead, h, c), (rest[0], h, c)]
    for s in rest[1:] + [last]:
        order += [(s, h, c) for h, c in chunks]

    todo = [functools.partial(scale_weights, i) for i in range(2 * tiles)]
    for _ in range(BEFORE):
        todo.pop(0)()
    own = pltpu.make_async_copy(tx.at[quad], rx.at[me], load_sem.at[0])
    own.start()

    pl.semaphore_wait(barrier, n - 1)
    local_chunks = list(chunks)
    behind = []

    def local_chunk():
        h, c = local_chunks.pop(0)
        send_quad(0, h, c, tx.at[quad, h, c])
        behind.append((0, h, c))

    for i in range(WINDOW):
        send_z(*order[i])
        if local_chunks:
            local_chunk()
    while todo:
        todo.pop(0)()
    own.wait()

    left = {}
    for s in range(quads):
        for h in range(2):
            left[s, h] = parts
    issued = [WINDOW]

    def queue(s, halves):
        todo.append(functools.partial(arrived_all, s, halves))
        if quads <= 4:
            todo.extend(functools.partial(compute, s, halves, t) for t in range(tiles))
        else:
            todo.append(lambda: pl.loop(0, tiles)(functools.partial(compute, s, halves)))
        todo.append(functools.partial(send_back, s, halves))

    def take_y():
        s, h, c = behind.pop(0)
        arrived_y(s, h, c)
        left[s, h] -= 1
        if left[s, h] == 0:
            if left[s, 1 - h] == 0:
                queue(s, (0, 1))

    for i, event in enumerate(order):
        work = len(todo)
        arrived_z(*event)
        behind.append(event)
        while issued[0] < len(order) and issued[0] <= i + WINDOW:
            send_z(*order[issued[0]])
            issued[0] += 1
        if local_chunks:
            local_chunk()
        while len(behind) > LAG:
            take_y()
        for _ in range(min(work, 3)):
            todo.pop(0)()
    while behind:
        take_y()
        if todo:
            todo.pop(0)()
    while todo:
        todo.pop(0)()
    for s in range(quads):
        finish(s)
    wait_for(tx.at[pl.ds(0, quads - 1)], sent.at[0])
    for kind in (1, 2, 3):
        wait_for(tx, sent.at[kind])
    wait_for(hid.at[pl.ds(0, n - 1)], sent.at[4])


def local(n, ids, prob, scale, tokens, gate_up):
    quads = n // SPLIT
    parts = max(1, 8 // quads)
    count, depth = tokens.shape
    tiles = gate_up.shape[1] // QB
    dma = pltpu.SemaphoreType.DMA
    vmem = pl.BlockSpec(memory_space=pltpu.VMEM)
    hbm = pl.BlockSpec(memory_space=pl.ANY)
    chunk = (2, parts, HALF, depth // parts)
    params = dict(vmem_limit_bytes=56 * 1024 * 1024)
    return pl.pallas_call(
        functools.partial(kernel, n, parts),
        out_shape=jax.ShapeDtypeStruct((CAP, n * tiles * QB), BF16),
        in_specs=[vmem, vmem, pl.BlockSpec(memory_space=pltpu.SMEM), hbm, hbm],
        out_specs=vmem,
        scratch_shapes=[
            pltpu.VMEM((count, depth), BF16),
            pltpu.VMEM((tiles, 2 * QB, depth), BF16),
            pltpu.VMEM((quads,) + chunk, BF16),
            pltpu.VMEM((n,) + chunk, BF16),
            pltpu.VMEM((n, 2, tiles, HALF, QB), BF16),
            pltpu.VMEM((n, 2, tiles, HALF, QB), BF16),
            pltpu.VMEM((quads * CAP, QB), F32),
            dma((1 + 2 * tiles,)),
            dma((5,)),
            dma((quads, 2, parts)),
            dma((quads, 2, parts)),
            dma((quads, 2)),
            dma((quads, 2)),
            dma((quads,)),
        ],
        compiler_params=pltpu.CompilerParams(collective_id=0, has_side_effects=True, **params),
        cost_estimate=pl.CostEstimate(
            flops=2 * n * CAP * 2 * tiles * QB * depth, bytes_accessed=10 ** 7, transcendentals=0),
    )(ids.T, prob.T, scale.transpose(1, 0, 2), tokens, gate_up)


def solution(mesh):
    n = mesh.shape["blk"]
    placed = (
        P(("groups", "blk"), None),
        P(("groups", "blk"), None),
        P(("groups", "blk"), None),
        P(None, "blk", None),
        P(None, "blk", None),
    )

    def body(tokens, expert_ids, route_prob, gate_up, block_scale):
        return local(n, expert_ids, route_prob, block_scale, tokens, gate_up)

    return jax.shard_map(
        body, mesh=mesh, in_specs=placed, out_specs=P(("groups", "blk"), None), check_vma=False
    )
```
